32 devices in a mesh: dp: 4 (over y, core), expert: 8 (over z, x).
Axes of the slice: x: 2, y: 2, z: 4, core: 2. Of those that a mesh axis runs over, the one named last changes fastest.
Arguments:
- tokens: bfloat16 [4096, 7168], P(('dp', 'expert')), may hold values from -6 to 6
- chosen: int32 [8, 288], replicated, may hold values from 0 to 4095, as said below
- combine_fixed: int32 [8, 288], replicated, may hold values from 6554 to 65535
- w_gate: bfloat16 [8, 7168, 2048], P('expert', None, 'dp'), may hold values from -0.0625 to 0.0625
- w_up: bfloat16 [8, 7168, 2048], P('expert', None, 'dp'), may hold values from -0.0625 to 0.0625
- w_down: bfloat16 [8, 2048, 7168], P('expert', 'dp'), may hold values from -0.125 to 0.125
Outputs:
- mixed: bfloat16 [4096, 7168], P(('dp', 'expert'))
The draws below stay inside these ranges and needn't reach their ends.
Inputs may be any that keep to these rules, and one draw needn't show every extreme that they name: `chosen`: in each row the 288 token numbers differ. Call tokens k * 128 to (k + 1) * 128 - 1 the tokens of device k: a row holds at most 18 tokens of one device, and exactly 18 of some device.
All inputs are finite; a program needn't handle non-finite values.
Results may differ from the reference program's by a relative error of at most 0.015.
Values may be sent and summed in bfloat16 or wider, within the bound.
A program may use at most 128 MiB of HBM per device.

```python
import jax
import jax.numpy as jnp
from jax import lax

D = 7168
HIDDEN_SIZE = 2048
TOK_DEV = 128
CAP = 288
EXPERTS = 8
HSLICE = 512
WORD_COUNT_ALL = 4096
SLOT = 18


def draw_chosen(key, part):
    worker_ordinal = WORD_COUNT_ALL // TOK_DEV

    def one_expert(derived_seed_handle):
        ordering_seed_handle, loaded_seed_handle, extra_seed_handle, perturb_seed_handle = jax.random.split(derived_seed_handle, 4)
        rank_keys = jax.random.split(ordering_seed_handle, worker_ordinal)
        ranks = jax.vmap(lambda k: jax.random.permutation(k, TOK_DEV))(rank_keys)
        eligible = ranks < SLOT
        loaded_worker = jax.random.randint(loaded_seed_handle, (), 0, worker_ordinal)
        logit_increment = jax.random.randint(extra_seed_handle, (worker_ordinal,), 0, 8) * 128
        logit_increment = jnp.where(jnp.arange(worker_ordinal) == loaded_worker, 4096, logit_increment)
        logit_perturbation = jax.random.randint(perturb_seed_handle, (worker_ordinal, TOK_DEV), 0, 1024)
        sequence_item_positions = jnp.arange(WORD_COUNT_ALL, dtype=jnp.int32).reshape(worker_ordinal, TOK_DEV)
        gating_logit_matrix = (logit_perturbation + logit_increment[:, None]) * WORD_COUNT_ALL + sequence_item_positions
        gating_logit_matrix = jnp.where(eligible, gating_logit_matrix, -1).reshape(-1)
        top_values, top_ids = lax.top_k(gating_logit_matrix, CAP)
        return top_ids.astype(jnp.int32)
    expert_keys = jax.random.split(jax.random.fold_in(key, 17), EXPERTS)
    return jax.vmap(one_expert)(expert_keys)


def with_ends(drawn, key, smallest, largest):
    longest = drawn.shape.index(max(drawn.shape))
    spots = []
    for shift in (0, 1):
        where = [jax.random.randint(jax.random.fold_in(key, axis), (), 0, length) for axis, length in enumerate(drawn.shape)]
        where[longest] = (where[longest] + shift) % drawn.shape[longest]
        spots.append(tuple(where))
    return drawn.at[spots[0]].set(smallest).at[spots[1]].set(largest)


def level_of(rng, dims, cuts, smallest, high):
    loudness, own = 1.0, jax.random.fold_in(rng, 6)
    for dim, parts in cuts:
        heights = jnp.exp(jax.random.uniform(jax.random.fold_in(own, dim), (parts,), jnp.float32, smallest / len(cuts), high / len(cuts)))
        loudness = loudness * jnp.repeat(heights, dims[dim] // parts).reshape([-1 if axis == dim else 1 for axis in range(len(dims))])
    return loudness


def normal_values(rng, dims, spread, limit, cuts=(), kind=jnp.bfloat16):
    array = spread * jax.random.normal(rng, dims, jnp.float32)
    if cuts:
        array = array * level_of(rng, dims, cuts, -0.22, 0.18)
    return jnp.clip(array, -limit, limit).astype(kind)


def setup_inputs(seed: int = 0) -> dict:
    streams_of = jax.random.split(jax.random.key(seed), 7)
    return {
        "tokens": normal_values(streams_of[0], (WORD_COUNT_ALL, D), 1.0, 6.0, ((0, 32),)),
        "chosen": draw_chosen(jax.random.fold_in(streams_of[6], 71), 0),
        "combine_fixed": with_ends(jax.random.randint(streams_of[2], (EXPERTS, CAP), 6554, 65536), jax.random.fold_in(streams_of[2], 1), 6554, 65535).astype(jnp.int32),
        "w_gate": normal_values(streams_of[3], (EXPERTS, D, HIDDEN_SIZE), D ** -0.5, 0.0625, ((0, 8), (2, 4))),
        "w_up": normal_values(streams_of[4], (EXPERTS, D, HIDDEN_SIZE), D ** -0.5, 0.0625, ((0, 8), (2, 4))),
        "w_down": normal_values(streams_of[5], (EXPERTS, HIDDEN_SIZE, D), HIDDEN_SIZE ** -0.5, 0.125, ((0, 8), (1, 4))),
    }


def reference(tokens, chosen, combine_fixed, w_gate, w_up, w_down):
    start_sum = jnp.zeros((WORD_COUNT_ALL, D), jnp.float32)

    def expert_step(expert_id, totals):
        picked_ids = chosen[expert_id]
        picked = jnp.take(tokens, picked_ids, axis=0)
        gate_act = jnp.dot(picked, w_gate[expert_id], preferred_element_type=jnp.float32)
        up_act = jnp.dot(picked, w_up[expert_id], preferred_element_type=jnp.float32)
        hidden = (jax.nn.silu(gate_act) * up_act).astype(jnp.bfloat16)
        down_rows = w_down[expert_id]
        result = jnp.zeros((CAP, D), jnp.float32)
        for piece in range(HIDDEN_SIZE // HSLICE):
            part = jnp.dot(hidden[:, piece * HSLICE:(piece + 1) * HSLICE],
                           down_rows[piece * HSLICE:(piece + 1) * HSLICE],
                           preferred_element_type=jnp.float32).astype(jnp.bfloat16)
            result = result + part.astype(jnp.float32)
        weights_row = combine_fixed[expert_id].astype(jnp.float32) / 65536.0
        return totals.at[picked_ids].add(weights_row[:, None] * result)

    totals = lax.fori_loop(0, EXPERTS, expert_step, start_sum)
    return totals.astype(jnp.bfloat16)
```

```python
import jax
import jax.numpy as jnp
from jax import lax
from jax.sharding import Mesh, PartitionSpec as P

BF = jnp.bfloat16
F32 = jnp.float32


def tables(chosen, combine_fixed, tok, dp, ea, eb):
    n = dp * ea * eb
    experts, cap = chosen.shape
    slot = min(tok, max(4, 2 * cap // n))
    r1 = -(-ea * slot // 16) * 16
    r2 = -(-dp * eb * slot // 16) * 16
    my_d, my_a, my_b = (lax.axis_index(k) for k in ("dp", "ea", "eb"))
    me = (my_d * ea + my_a) * eb + my_b
    owners = chosen // tok
    pos = jnp.arange(cap, dtype=jnp.int32)
    same = (owners[:, :, None] == owners[:, None, :]) & (pos[None, None, :] < pos[None, :, None])
    ranks = jnp.sum(same.astype(jnp.int32), axis=2)
    local = chosen - owners * tok
    match = ((owners == me)[:, None, :]) & (
        ranks[:, None, :] == jnp.arange(slot, dtype=jnp.int32)[None, :, None]
    )
    source = jnp.sum(jnp.where(match, local[:, None, :] + 1, 0), axis=2) - 1
    sel = (source[:, :, None] == jnp.arange(tok, dtype=jnp.int32)).astype(BF)
    sel = sel.reshape(ea, eb, slot, tok).transpose(1, 0, 2, 3).reshape(eb, ea * slot, tok)
    sel = jnp.pad(sel, ((0, 0), (0, r1 - ea * slot), (0, 0)))
    mine = my_a * eb + my_b
    own = lax.dynamic_index_in_dim(owners, mine, 0, keepdims=False)
    rank = lax.dynamic_index_in_dim(ranks, mine, 0, keepdims=False)
    weight = lax.dynamic_index_in_dim(combine_fixed, mine, 0, keepdims=False)
    weight = weight.astype(F32)[:, None] / 65536.0
    plane = (own // (ea * eb)) * eb + own % eb
    row_a = (own // eb) % ea
    where = plane * slot + rank
    pick = (row_a[None, :] == jnp.arange(ea, dtype=jnp.int32)[:, None])[:, :, None] & (
        where[None, :, None] == jnp.arange(r2, dtype=jnp.int32)
    )
    pick = pick.astype(BF)
    out_row = jnp.arange(r2, dtype=jnp.int32)[None, :, None]
    in_row = jnp.arange(dp * eb * r1, dtype=jnp.int32)[None, None, :]
    which = jnp.arange(ea, dtype=jnp.int32)[:, None, None]
    wanted = (out_row // slot) * r1 + which * slot + out_row % slot
    turn = ((in_row == wanted) & (out_row < dp * eb * slot)).astype(BF)
    return sel, pick, weight, turn, r1, r2


def dot(a, b):
    return jnp.dot(a, b, preferred_element_type=F32)


def shards(tokens, chosen, combine_fixed, w_gate, w_up, w_down):
    dp, ea, eb = (lax.axis_size(k) for k in ("dp", "ea", "eb"))
    tok, width = tokens.shape
    cap = chosen.shape[1]
    quarter = width // dp
    group = dp * eb
    sel, pick, weight, turn, r1, r2 = tables(chosen, combine_fixed, tok, dp, ea, eb)
    send = dot(sel.reshape(eb * r1, tok), tokens).astype(BF)
    send = send.reshape(eb, r1, dp, quarter).transpose(2, 0, 1, 3).reshape(group, r1, quarter)
    got = lax.all_to_all(send, ("dp", "eb"), 0, 0, tiled=True).reshape(group * r1, quarter)
    send = dot(turn.reshape(ea * r2, group * r1), got).astype(BF).reshape(ea, r2, quarter)
    got = lax.all_to_all(send, "ea", 0, 0, tiled=True).reshape(ea * r2, quarter)
    picked = dot(pick.transpose(1, 0, 2).reshape(cap, ea * r2), got).astype(BF)
    picked = lax.all_gather(picked, "dp", axis=1, tiled=True)
    gate = dot(picked, w_gate[0])
    up = dot(picked, w_up[0])
    hidden = (jax.nn.silu(gate) * up).astype(BF)
    part = dot(hidden, w_down[0]).astype(BF)
    total = lax.psum_scatter(part, "dp", scatter_dimension=1, tiled=True)
    total = (total.astype(F32) * weight).astype(BF)
    send = jnp.einsum("apr,pq->arq", pick, total, preferred_element_type=F32).astype(BF)
    got = lax.all_to_all(send, "ea", 0, 0, tiled=True)
    send = jnp.einsum("arg,arq->gq", turn, got, preferred_element_type=F32).astype(BF)
    got = lax.all_to_all(send.reshape(group, r1, quarter), ("dp", "eb"), 0, 0, tiled=True)
    mixed = jnp.einsum(
        "brt,dbrq->tdq", sel, got.reshape(dp, eb, r1, quarter), preferred_element_type=F32
    )
    return mixed.reshape(tok, width).astype(BF)


def solution(mesh):
    dp, experts = mesh.devices.shape
    finer = Mesh(mesh.devices.reshape(dp, experts // 2, 2), ("dp", "ea", "eb"))
    ex = ("ea", "eb")
    in_specs = (
        P(("dp",) + ex, None), P(), P(),
        P(ex, None, "dp"), P(ex, None, "dp"), P(ex, "dp", None),
    )
    return jax.shard_map(
        shards, mesh=finer, in_specs=in_specs, out_specs=P(("dp",) + ex, None), check_vma=False
    )
```

```python
import functools

import jax
import jax.numpy as jnp
from jax import lax
from jax.experimental import pallas as pl
from jax.experimental.pallas import tpu as pltpu
from jax.sharding import Mesh, PartitionSpec as P

BF = jnp.bfloat16
F32 = jnp.float32


def tables(chosen, combine_fixed, tok, dp, ea, eb):
    n = dp * ea * eb
    experts, cap = chosen.shape
    slot = min(tok, max(4, 2 * cap // n))
    r1 = -(-ea * slot // 16) * 16
    r2 = -(-dp * eb * slot // 16) * 16
    my_d, my_a, my_b = (lax.axis_index(k) for k in ("dp", "ea", "eb"))
    me = (my_d * ea + my_a) * eb + my_b
    owners = chosen // tok
    pos = jnp.arange(cap, dtype=jnp.int32)
    same = (owners[:, :, None] == owners[:, None, :]) & (pos[None, None, :] < pos[None, :, None])
    ranks = jnp.sum(same.astype(jnp.int32), axis=2)
    local = chosen - owners * tok
    match = ((owners == me)[:, None, :]) & (
        ranks[:, None, :] == jnp.arange(slot, dtype=jnp.int32)[None, :, None]
    )
    source = jnp.sum(jnp.where(match, local[:, None, :] + 1, 0), axis=2) - 1
    sel = (source[:, :, None] == jnp.arange(tok, dtype=jnp.int32)).astype(BF)
    sel = sel.reshape(ea, eb, slot, tok).transpose(1, 0, 2, 3).reshape(eb, ea * slot, tok)
    sel = jnp.pad(sel, ((0, 0), (0, r1 - ea * slot), (0, 0)))
    mine = my_a * eb + my_b
    own = lax.dynamic_index_in_dim(owners, mine, 0, keepdims=False)
    rank = lax.dynamic_index_in_dim(ranks, mine, 0, keepdims=False)
    weight = lax.dynamic_index_in_dim(combine_fixed, mine, 0, keepdims=False)
    weight = weight.astype(F32)[:, None] / 65536.0
    plane = (own // (ea * eb)) * eb + own % eb
    row_a = (own // eb) % ea
    where = plane * slot + rank
    pick = (row_a[None, :] == jnp.arange(ea, dtype=jnp.int32)[:, None])[:, :, None] & (
        where[None, :, None] == jnp.arange(r2, dtype=jnp.int32)
    )
    pick = pick.astype(BF)
    out_row = jnp.arange(r2, dtype=jnp.int32)[None, :, None]
    in_row = jnp.arange(dp * eb * r1, dtype=jnp.int32)[None, None, :]
    which = jnp.arange(ea, dtype=jnp.int32)[:, None, None]
    wanted = (out_row // slot) * r1 + which * slot + out_row % slot
    turn = ((in_row == wanted) & (out_row < dp * eb * slot)).astype(BF)
    return sel, pick, weight, turn, r1, r2


def dot(a, b):
    return jnp.dot(a, b, preferred_element_type=F32)


def remote(src, dst, send_sem, recv_sem, target):
    return pltpu.make_async_remote_copy(
        src_ref=src, dst_ref=dst, send_sem=send_sem, recv_sem=recv_sem,
        device_id=target, device_id_type=pl.DeviceIdType.MESH,
    )


def kernel(
    dp, ea, eb, chunks,
    tokens, sel, selt, pick, pickt, weight, turn, turnt, w_gate, w_up, w_down,
    out,
    wg, wu, wd, rows1, in1, in4, rows2, in2, in3, picked, gate, up, hidden,
    pair_out, pair_in, far_out, far_in, total,
    w_sem, s1, v1, s4, v4, s2, v2, s3, v3, s_far, s_pair, v_pick, s_sum, v_sum, s_ys, v_ys,
):
    d, a, b = (lax.axis_index(k) for k in ("dp", "ea", "eb"))
    group = dp * eb
    half = dp // 2
    g = d * eb + b
    sibling = d + 1 - 2 * lax.rem(d, 2)
    cap, cols = total.shape[1:]

    def peer(i):
        p = lax.rem(g + i, group)
        return p, (p // eb, a, lax.rem(p, eb))

    def along(i):
        e = lax.rem(a + i, ea)
        return e, (d, e, b)

    def far(j):
        return lax.rem(d + 2 * j, dp)

    def block(q, c):
        return pl.ds(pl.multiple_of((q * chunks + c) * cols, 128), cols)

    loads = [
        pltpu.make_async_copy(src.at[0], dst, w_sem.at[k])
        for k, (src, dst) in enumerate(((w_gate, wg), (w_up, wu), (w_down, wd)))
    ]
    for load in loads:
        load.start()

    barrier = pltpu.get_barrier_semaphore()

    @pl.loop(1, group)
    def _(i):
        pl.semaphore_signal(barrier, inc=1, device_id=peer(i)[1], device_id_type=pl.DeviceIdType.MESH)

    @pl.loop(1, ea)
    def _(i):
        pl.semaphore_signal(barrier, inc=1, device_id=along(i)[1], device_id_type=pl.DeviceIdType.MESH)

    pl.semaphore_wait(barrier, group + ea - 2)

    def sent1(c, i):
        p, target = peer(i)
        return remote(rows1.at[c, p], in1.at[c, g], s1.at[c, p], v1.at[c, g], target)

    def came1(c, i):
        p, target = peer(i)
        return remote(rows1.at[c, p], in1.at[c, p], s1.at[c, p], v1.at[c, p], target)

    for c in range(chunks):
        @pl.loop(1, group)
        def _(i):
            p, _ = peer(i)
            rows1[c, p] = dot(sel[lax.rem(p, eb)], tokens[:, block(p // eb, c)]).astype(BF)
            sent1(c, i).start()

        in1[c, g] = dot(sel[b], tokens[:, block(d, c)]).astype(BF)

    def sent2(c, i):
        e, target = along(i)
        return remote(rows2.at[c, e], in2.at[c, a], s2.at[c, e], v2.at[c, a], target)

    def came2(c, i):
        e, target = along(i)
        return remote(rows2.at[c, e], in2.at[c, e], s2.at[c, e], v2.at[c, e], target)

    for c in range(chunks):
        @pl.loop(1, group)
        def _(i):
            came1(c, i).wait_recv()

        @pl.loop(1, ea)
        def _(i):
            e, _ = along(i)
            rows2[c, e] = dot(turn[e], in1[c].reshape(-1, cols)).astype(BF)
            sent2(c, i).start()

        in2[c, a] = dot(turn[a], in1[c].reshape(-1, cols)).astype(BF)

    def to_far(c, j):
        mine = d * chunks + c
        return remote(picked.at[mine], picked.at[mine], s_far.at[c, j], v_pick.at[mine], (far(j), a, b))

    def to_pair(c, j):
        slot = far(j) * chunks + c
        return remote(picked.at[slot], picked.at[slot], s_pair.at[c, j], v_pick.at[slot], (sibling, a, b))

    def arrival(q, c):
        slot = q * chunks + c
        return remote(picked.at[slot], picked.at[slot], s_pair.at[0, 0], v_pick.at[slot], (sibling, a, b))

    def project(q, c):
        slot = q * chunks + c
        x = picked[slot]
        where = pl.ds(pl.multiple_of(slot * cols, 128), cols)
        gate[...] += dot(x, wg[where, :])
        up[...] += dot(x, wu[where, :])

    gate[...] = jnp.zeros_like(gate)
    up[...] = jnp.zeros_like(up)
    for c in range(chunks):
        @pl.loop(1, ea)
        def _(i):
            came2(c, i).wait_recv()

        x = dot(pick[0], in2[c, 0])
        for e in range(1, ea):
            x += dot(pick[e], in2[c, e])
        picked[d * chunks + c] = x.astype(BF)

        @pl.loop(1, half)
        def _(j):
            to_far(c, j).start()

        to_pair(c, 0).start()
    loads[0].wait()
    loads[1].wait()

    @pl.loop(0, chunks)
    def _(c):
        project(d, c)

    @pl.loop(1, half)
    def _(j):
        @pl.loop(0, chunks)
        def _(c):
            arrival(far(j), c).wait_recv()
            to_pair(c, j).start()
            project(far(j), c)

    @pl.loop(0, half)
    def _(j):
        @pl.loop(0, chunks)
        def _(c):
            q = lax.rem(sibling + 2 * j, dp)
            arrival(q, c).wait_recv()
            project(q, c)

    v = gate[...]
    hidden[...] = (v / (1.0 + jnp.exp(-v)) * up[...]).astype(BF)
    loads[2].wait()

    def pair_sum(c, j):
        return remote(pair_out.at[c, j], pair_in.at[c, j], s_sum.at[c, j], v_sum.at[c, j], (sibling, a, b))

    def far_sum(c, j):
        return remote(far_out.at[c, j], far_in.at[c, j], s_ys.at[c, j], v_ys.at[c, j], (far(j), a, b))

    def part(q, c):
        return dot(hidden[...], wd[:, block(q, c)])

    @pl.loop(1, half + 1)
    def _(k):
        j = lax.rem(k, half)

        @pl.loop(0, chunks)
        def _(c):
            pair_out[c, j] = part(lax.rem(sibling + 2 * j, dp), c).astype(BF)
            pair_sum(c, j).start()

    @pl.loop(1, half)
    def _(j):
        @pl.loop(0, chunks)
        def _(c):
            mine = part(far(j), c)
            pair_sum(c, j).wait_recv()
            far_out[c, j] = (mine + pair_in[c, j].astype(F32)).astype(BF)
            far_sum(c, j).start()

    def sent3(c, i):
        e, target = along(i)
        return remote(rows2.at[c, e], in3.at[c, a], s3.at[c, e], v3.at[c, a], target)

    def came3(c, i):
        e, target = along(i)
        return remote(rows2.at[c, e], in3.at[c, e], s3.at[c, e], v3.at[c, e], target)

    for c in range(chunks):
        mine = part(d, c)
        pair_sum(c, 0).wait_recv()
        mine += pair_in[c, 0].astype(F32)
        for j in range(1, half):
            far_sum(c, j).wait_recv()
            mine += far_in[c, j].astype(F32)
        total[c] = (mine * weight[...]).astype(BF)

        @pl.loop(1, ea)
        def _(i):
            e, _ = along(i)
            sent2(c, i).wait_send()
            rows2[c, e] = dot(pickt[e], total[c]).astype(BF)
            sent3(c, i).start()

        in3[c, a] = dot(pickt[a], total[c]).astype(BF)

    def sent4(c, i):
        p, target = peer(i)
        return remote(rows1.at[c, p], in4.at[c, g], s4.at[c, p], v4.at[c, g], target)

    def came4(c, i):
        p, target = peer(i)
        return remote(rows1.at[c, p], in4.at[c, p], s4.at[c, p], v4.at[c, p], target)

    for c in range(chunks):
        @pl.loop(1, ea)
        def _(i):
            came3(c, i).wait_recv()

        @pl.loop(1, group)
        def _(i):
            p, _ = peer(i)
            sent1(c, i).wait_send()
            rows1[c, p] = dot(turnt[p], in3[c].reshape(-1, cols)).astype(BF)
            sent4(c, i).start()

        in4[c, g] = dot(turnt[g], in3[c].reshape(-1, cols)).astype(BF)

    for c in range(chunks):
        @pl.loop(1, group)
        def _(i):
            came4(c, i).wait_recv()

        @pl.loop(0, dp)
        def _(q):
            x = dot(selt[0], in4[c, q * eb])
            for k in range(1, eb):
                x += dot(selt[k], in4[c, q * eb + k])
            out[:, block(q, c)] = x.astype(BF)

    @pl.loop(0, chunks)
    def _(c):
        @pl.loop(1, group)
        def _(i):
            sent4(c, i).wait_send()

        @pl.loop(1, ea)
        def _(i):
            sent3(c, i).wait_send()

        @pl.loop(1, half)
        def _(j):
            to_far(c, j).wait_send()
            far_sum(c, j).wait_send()

        @pl.loop(0, half)
        def _(j):
            to_pair(c, j).wait_send()
            pair_sum(c, j).wait_send()


def shards(tokens, chosen, combine_fixed, w_gate, w_up, w_down):
    dp, ea, eb = (lax.axis_size(k) for k in ("dp", "ea", "eb"))
    tok, width = tokens.shape
    cap = chosen.shape[1]
    units = w_gate.shape[2]
    quarter = width // dp
    group = dp * eb
    half = dp // 2
    chunks = 2 if quarter % 256 == 0 else 1
    cols = quarter // chunks
    sel, pick, weight, turn, r1, r2 = tables(chosen, combine_fixed, tok, dp, ea, eb)
    selt = sel.transpose(0, 2, 1)
    pickt = pick.transpose(0, 2, 1)
    turnt = turn.reshape(ea, r2, group, r1).transpose(2, 3, 0, 1).reshape(group, r1, ea * r2)
    vmem = pl.BlockSpec(memory_space=pltpu.VMEM)
    hbm = pl.BlockSpec(memory_space=pl.ANY)
    sems = lambda *shape: pltpu.SemaphoreType.DMA(shape)
    return pl.pallas_call(
        functools.partial(kernel, dp, ea, eb, chunks),
        out_shape=jax.ShapeDtypeStruct((tok, width), BF),
        in_specs=[vmem] * 8 + [hbm] * 3,
        out_specs=vmem,
        scratch_shapes=[
            pltpu.VMEM((width, units), BF), pltpu.VMEM((width, units), BF), pltpu.VMEM((units, width), BF),
            pltpu.VMEM((chunks, group, r1, cols), BF),
            pltpu.VMEM((chunks, group, r1, cols), BF),
            pltpu.VMEM((chunks, group, r1, cols), BF),
            pltpu.VMEM((chunks, ea, r2, cols), BF),
            pltpu.VMEM((chunks, ea, r2, cols), BF),
            pltpu.VMEM((chunks, ea, r2, cols), BF),
            pltpu.VMEM((dp * chunks, cap, cols), BF),
            pltpu.VMEM((cap, units), F32), pltpu.VMEM((cap, units), F32), pltpu.VMEM((cap, units), BF),
            pltpu.VMEM((chunks, half, cap, cols), BF), pltpu.VMEM((chunks, half, cap, cols), BF),
            pltpu.VMEM((chunks, half, cap, cols), BF), pltpu.VMEM((chunks, half, cap, cols), BF),
            pltpu.VMEM((chunks, cap, cols), BF),
            sems(3),
            sems(chunks, group), sems(chunks, group), sems(chunks, group), sems(chunks, group),
            sems(chunks, ea), sems(chunks, ea), sems(chunks, ea), sems(chunks, ea),
            sems(chunks, half), sems(chunks, half), sems(dp * chunks),
            sems(chunks, half), sems(chunks, half), sems(chunks, half), sems(chunks, half),
        ],
        compiler_params=pltpu.CompilerParams(
            collective_id=0, has_side_effects=True, vmem_limit_bytes=62 * 1024 * 1024
        ),
    )(tokens, sel, selt, pick, pickt, weight, turn, turnt, w_gate, w_up, w_down)


def solution(mesh):
    dp, experts = mesh.devices.shape
    finer = Mesh(mesh.devices.reshape(dp, experts // 2, 2), ("dp", "ea", "eb"))
    ex = ("ea", "eb")
    in_specs = (
        P(("dp",) + ex, None), P(), P(),
        P(ex, None, "dp"), P(ex, None, "dp"), P(ex, "dp", None),
    )
    return jax.shard_map(
        shards, mesh=finer, in_specs=in_specs, out_specs=P(("dp",) + ex, None), check_vma=False
    )
```

```python
import functools

import jax
import jax.numpy as jnp
import numpy as np
from jax import lax
from jax.experimental import pallas as pl
from jax.experimental.pallas import tpu as pltpu
from jax.sharding import Mesh, PartitionSpec as P

BF = jnp.bfloat16
F32 = jnp.float32


def tables(chosen, combine_fixed, tok, dp, ea, eb):
    n = dp * ea * eb
    experts, cap = chosen.shape
    slot = min(tok, max(4, 2 * cap // n))
    r1 = -(-ea * slot // 16) * 16
    r2 = -(-dp * eb * slot // 16) * 16
    my_d, my_a, my_b = (lax.axis_index(k) for k in ("dp", "ea", "eb"))
    me = (my_d * ea + my_a) * eb + my_b
    owners = chosen // tok
    pos = jnp.arange(cap, dtype=jnp.int32)
    same = (owners[:, :, None] == owners[:, None, :]) & (pos[None, None, :] < pos[None, :, None])
    ranks = jnp.sum(same.astype(jnp.int32), axis=2)
    local = chosen - owners * tok
    match = ((owners == me)[:, None, :]) & (
        ranks[:, None, :] == jnp.arange(slot, dtype=jnp.int32)[None, :, None]
    )
    source = jnp.sum(jnp.where(match, local[:, None, :] + 1, 0), axis=2) - 1
    sel = (source[:, :, None] == jnp.arange(tok, dtype=jnp.int32)).astype(BF)
    sel = sel.reshape(ea, eb, slot, tok).transpose(1, 0, 2, 3).reshape(eb, ea * slot, tok)
    sel = jnp.pad(sel, ((0, 0), (0, r1 - ea * slot), (0, 0)))
    mine = my_a * eb + my_b
    own = lax.dynamic_index_in_dim(owners, mine, 0, keepdims=False)
    rank = lax.dynamic_index_in_dim(ranks, mine, 0, keepdims=False)
    weight = lax.dynamic_index_in_dim(combine_fixed, mine, 0, keepdims=False)
    weight = weight.astype(F32)[:, None] / 65536.0
    plane = (own // (ea * eb)) * eb + own % eb
    row_a = (own // eb) % ea
    where = plane * slot + rank
    pick = (row_a[None, :] == jnp.arange(ea, dtype=jnp.int32)[:, None])[:, :, None] & (
        where[None, :, None] == jnp.arange(r2, dtype=jnp.int32)
    )
    pick = pick.astype(BF)
    out_row = np.arange(r2)[None, :, None]
    in_row = np.arange(dp * eb * r1)[None, None, :]
    which = np.arange(ea)[:, None, None]
    wanted = (out_row // slot) * r1 + which * slot + out_row % slot
    turn = ((in_row == wanted) & (out_row < dp * eb * slot)).astype(np.float32)
    return sel, pick, weight, turn, r1, r2


def dot(a, b):
    return jnp.dot(a, b, preferred_element_type=F32)


def remote(src, dst, send_sem, recv_sem, target):
    return pltpu.make_async_remote_copy(
        src_ref=src, dst_ref=dst, send_sem=send_sem, recv_sem=recv_sem,
        device_id=target, device_id_type=pl.DeviceIdType.MESH,
    )


def kernel(
    dp, ea, eb, chunks,
    tokens, sel, selt, pick, pickt, weight, turn, turnt, w_gate, w_up, w_down,
    out,
    wg, wu, wd, rows1, in1, in4, rows2, in2, in3, picked, gate, up, hidden,
    pair_out, pair_in, far_out, far_in, total,
    w_sem, s1, v1, s4, v4, s2, v2, s3, v3, s_far, s_pair, v_pick, s_sum, v_sum, s_ys, v_ys,
):
    d, a, b = (lax.axis_index(k) for k in ("dp", "ea", "eb"))
    group = dp * eb
    half = dp // 2
    g = d * eb + b
    sibling = d + 1 - 2 * lax.rem(d, 2)
    cap, cols = total.shape[1:]

    def peer(i):
        p = lax.rem(g + i, group)
        return p, (p // eb, a, lax.rem(p, eb))

    def along(i):
        e = lax.rem(a + i, ea)
        return e, (d, e, b)

    def far(j):
        return lax.rem(d + 2 * j, dp)

    def block(q, c):
        return pl.ds(pl.multiple_of((q * chunks + c) * cols, 128), cols)

    loads = [
        pltpu.make_async_copy(src.at[0], dst, w_sem.at[k])
        for k, (src, dst) in enumerate(((w_gate, wg), (w_up, wu), (w_down, wd)))
    ]
    for load in loads:
        load.start()

    barrier = pltpu.get_barrier_semaphore()

    @pl.loop(1, group)
    def _(i):
        pl.semaphore_signal(barrier, inc=1, device_id=peer(i)[1], device_id_type=pl.DeviceIdType.MESH)

    @pl.loop(1, ea)
    def _(i):
        pl.semaphore_signal(barrier, inc=1, device_id=along(i)[1], device_id_type=pl.DeviceIdType.MESH)

    pl.semaphore_wait(barrier, group + ea - 2)

    def sent1(c, i):
        p, target = peer(i)
        return remote(rows1.at[c, p], in1.at[c, g], s1.at[c, p], v1.at[c, g], target)

    def came1(c, i):
        p, target = peer(i)
        return remote(rows1.at[c, p], in1.at[c, p], s1.at[c, p], v1.at[c, p], target)

    @pl.loop(0, chunks)
    def _(c):
        @pl.loop(1, group)
        def _(i):
            p, _ = peer(i)
            rows1[c, p] = dot(sel[lax.rem(p, eb)], tokens[:, block(p // eb, c)]).astype(BF)
            sent1(c, i).start()

        in1[c, g] = dot(sel[b], tokens[:, block(d, c)]).astype(BF)

    def sent2(c, i):
        e, target = along(i)
        return remote(rows2.at[c, e], in2.at[c, a], s2.at[c, e], v2.at[c, a], target)

    def came2(c, i):
        e, target = along(i)
        return remote(rows2.at[c, e], in2.at[c, e], s2.at[c, e], v2.at[c, e], target)

    @pl.loop(0, chunks)
    def _(c):
        @pl.loop(1, group)
        def _(i):
            came1(c, i).wait_recv()

        @pl.loop(1, ea)
        def _(i):
            e, _ = along(i)
            rows2[c, e] = dot(turn[e], in1[c].reshape(-1, cols)).astype(BF)
            sent2(c, i).start()

        in2[c, a] = dot(turn[a], in1[c].reshape(-1, cols)).astype(BF)

    def to_far(c, j):
        mine = d * chunks + c
        return remote(picked.at[mine], picked.at[mine], s_far.at[c, j], v_pick.at[mine], (far(j), a, b))

    def to_pair(c, j):
        slot = far(j) * chunks + c
        return remote(picked.at[slot], picked.at[slot], s_pair.at[c, j], v_pick.at[slot], (sibling, a, b))

    def arrival(q, c):
        slot = q * chunks + c
        return remote(picked.at[slot], picked.at[slot], s_pair.at[0, 0], v_pick.at[slot], (sibling, a, b))

    def project(q, c):
        slot = q * chunks + c
        x = picked[slot]
        where = pl.ds(pl.multiple_of(slot * cols, 128), cols)
        gate[...] += dot(x, wg[where, :])
        up[...] += dot(x, wu[where, :])

    def pick_rows(c):
        @pl.loop(1, ea)
        def _(i):
            came2(c, i).wait_recv()

        x = dot(pick[0], in2[c, 0])
        for e in range(1, ea):
            x += dot(pick[e], in2[c, e])
        picked[d * chunks + c] = x.astype(BF)

        @pl.loop(1, half)
        def _(j):
            to_far(c, j).start()

        to_pair(c, 0).start()

    def pass_on(c):
        @pl.loop(1, half)
        def _(j):
            arrival(far(j), c).wait_recv()
            to_pair(c, j).start()
            project(far(j), c)

    def from_pair(c):
        @pl.loop(0, half)
        def _(j):
            q = lax.rem(sibling + 2 * j, dp)
            arrival(q, c).wait_recv()
            project(q, c)

    gate[...] = jnp.zeros_like(gate)
    up[...] = jnp.zeros_like(up)
    for step in range(chunks + 2):
        if step < chunks:
            pick_rows(step)
            if step == 0:
                loads[0].wait()
                loads[1].wait()
            project(d, step)
        if 1 <= step <= chunks:
            pass_on(step - 1)
        if step >= 2:
            from_pair(step - 2)

    v = gate[...]
    hidden[...] = (v / (1.0 + jnp.exp(-v)) * up[...]).astype(BF)
    loads[2].wait()

    def pair_sum(c, j):
        return remote(pair_out.at[c, j], pair_in.at[c, j], s_sum.at[c, j], v_sum.at[c, j], (sibling, a, b))

    def far_sum(c, j):
        return remote(far_out.at[c, j], far_in.at[c, j], s_ys.at[c, j], v_ys.at[c, j], (far(j), a, b))

    def part(q, c):
        return dot(hidden[...], wd[:, block(q, c)])

    @pl.loop(0, chunks)
    def _(c):
        @pl.loop(1, half + 1)
        def _(k):
            j = lax.rem(k, half)
            pair_out[c, j] = part(lax.rem(sibling + 2 * j, dp), c).astype(BF)
            pair_sum(c, j).start()

    @pl.loop(0, chunks)
    def _(c):
        @pl.loop(1, half)
        def _(j):
            mine = part(far(j), c)
            pair_sum(c, j).wait_recv()
            far_out[c, j] = (mine + pair_in[c, j].astype(F32)).astype(BF)
            far_sum(c, j).start()

    def sent3(c, i):
        e, target = along(i)
        return remote(rows2.at[c, e], in3.at[c, a], s3.at[c, e], v3.at[c, a], target)

    def came3(c, i):
        e, target = along(i)
        return remote(rows2.at[c, e], in3.at[c, e], s3.at[c, e], v3.at[c, e], target)

    @pl.loop(0, chunks)
    def _(c):
        mine = part(d, c)
        pair_sum(c, 0).wait_recv()
        mine += pair_in[c, 0].astype(F32)
        for j in range(1, half):
            far_sum(c, j).wait_recv()
            mine += far_in[c, j].astype(F32)
        total[c] = (mine * weight[...]).astype(BF)

        @pl.loop(1, ea)
        def _(i):
            e, _ = along(i)
            sent2(c, i).wait_send()
            rows2[c, e] = dot(pickt[e], total[c]).astype(BF)
            sent3(c, i).start()

        in3[c, a] = dot(pickt[a], total[c]).astype(BF)

    def sent4(c, i):
        p, target = peer(i)
        return remote(rows1.at[c, p], in4.at[c, g], s4.at[c, p], v4.at[c, g], target)

    def came4(c, i):
        p, target = peer(i)
        return remote(rows1.at[c, p], in4.at[c, p], s4.at[c, p], v4.at[c, p], target)

    @pl.loop(0, chunks)
    def _(c):
        @pl.loop(1, ea)
        def _(i):
            came3(c, i).wait_recv()

        @pl.loop(1, group)
        def _(i):
            p, _ = peer(i)
            sent1(c, i).wait_send()
            rows1[c, p] = dot(turnt[p], in3[c].reshape(-1, cols)).astype(BF)
            sent4(c, i).start()

        in4[c, g] = dot(turnt[g], in3[c].reshape(-1, cols)).astype(BF)

    @pl.loop(0, chunks)
    def _(c):
        @pl.loop(1, group)
        def _(i):
            came4(c, i).wait_recv()

        @pl.loop(0, dp)
        def _(q):
            x = dot(selt[0], in4[c, q * eb])
            for k in range(1, eb):
                x += dot(selt[k], in4[c, q * eb + k])
            out[:, block(q, c)] = x.astype(BF)

    @pl.loop(0, chunks)
    def _(c):
        @pl.loop(1, group)
        def _(i):
            sent4(c, i).wait_send()

        @pl.loop(1, ea)
        def _(i):
            sent3(c, i).wait_send()

        @pl.loop(1, half)
        def _(j):
            to_far(c, j).wait_send()
            far_sum(c, j).wait_send()

        @pl.loop(0, half)
        def _(j):
            to_pair(c, j).wait_send()
            pair_sum(c, j).wait_send()


def shards(tokens, chosen, combine_fixed, w_gate, w_up, w_down):
    dp, ea, eb = (lax.axis_size(k) for k in ("dp", "ea", "eb"))
    tok, width = tokens.shape
    cap = chosen.shape[1]
    units = w_gate.shape[2]
    quarter = width // dp
    group = dp * eb
    half = dp // 2
    chunks = next(k for k in (7, 2, 1) if quarter % (128 * k) == 0)
    cols = quarter // chunks
    sel, pick, weight, turn, r1, r2 = tables(chosen, combine_fixed, tok, dp, ea, eb)
    selt = sel.transpose(0, 2, 1)
    pickt = pick.transpose(0, 2, 1)
    turnt = turn.reshape(ea, r2, group, r1).transpose(2, 3, 0, 1).reshape(group, r1, ea * r2)
    turn, turnt = jnp.asarray(turn, BF), jnp.asarray(turnt, BF)
    vmem = pl.BlockSpec(memory_space=pltpu.VMEM)
    hbm = pl.BlockSpec(memory_space=pl.ANY)
    sems = lambda *shape: pltpu.SemaphoreType.DMA(shape)
    return pl.pallas_call(
        functools.partial(kernel, dp, ea, eb, chunks),
        out_shape=jax.ShapeDtypeStruct((tok, width), BF),
        in_specs=[vmem] * 8 + [hbm] * 3,
        out_specs=vmem,
        scratch_shapes=[
            pltpu.VMEM((width, units), BF), pltpu.VMEM((width, units), BF), pltpu.VMEM((units, width), BF),
            pltpu.VMEM((chunks, group, r1, cols), BF),
            pltpu.VMEM((chunks, group, r1, cols), BF),
            pltpu.VMEM((chunks, group, r1, cols), BF),
            pltpu.VMEM((chunks, ea, r2, cols), BF),
            pltpu.VMEM((chunks, ea, r2, cols), BF),
            pltpu.VMEM((chunks, ea, r2, cols), BF),
            pltpu.VMEM((dp * chunks, cap, cols), BF),
            pltpu.VMEM((cap, units), F32), pltpu.VMEM((cap, units), F32), pltpu.VMEM((cap, units), BF),
            pltpu.VMEM((chunks, half, cap, cols), BF), pltpu.VMEM((chunks, half, cap, cols), BF),
            pltpu.VMEM((chunks, half, cap, cols), BF), pltpu.VMEM((chunks, half, cap, cols), BF),
            pltpu.VMEM((chunks, cap, cols), BF),
            sems(3),
            sems(chunks, group), sems(chunks, group), sems(chunks, group), sems(chunks, group),
            sems(chunks, ea), sems(chunks, ea), sems(chunks, ea), sems(chunks, ea),
            sems(chunks, half), sems(chunks, half), sems(dp * chunks),
            sems(chunks, half), sems(chunks, half), sems(chunks, half), sems(chunks, half),
        ],
        compiler_params=pltpu.CompilerParams(
            collective_id=0, has_side_effects=True, vmem_limit_bytes=62 * 1024 * 1024
        ),
    )(tokens, sel, selt, pick, pickt, weight, turn, turnt, w_gate, w_up, w_down)


def solution(mesh):
    dp, experts = mesh.devices.shape
    finer = Mesh(mesh.devices.reshape(dp, experts // 2, 2), ("dp", "ea", "eb"))
    ex = ("ea", "eb")
    in_specs = (
        P(("dp",) + ex, None), P(), P(),
        P(ex, None, "dp"), P(ex, None, "dp"), P(ex, "dp", None),
    )
    return jax.shard_map(
        shards, mesh=finer, in_specs=in_specs, out_specs=P(("dp",) + ex, None), check_vma=False
    )
```
